32 devices in a mesh: nodes: 8 (over y, x, core), states: 4 (over z).
Axes of the slice: x: 2, y: 2, z: 4, core: 2. Of those that a mesh axis runs over, the one named last changes fastest.
Arguments:
- states_block: float32 [128, 4096], P('states', 'nodes'), may hold values from -6 to 6
- hamiltonian: bfloat16 [64, 64, 1728], P('nodes'), may hold values from -0.15625 to 0.15625
- offsets: int32 [64, 27], P('nodes'), may hold values from -4 to 4, as said below
- center: float32 [1], replicated, may hold values from -0.5 to 0.5
- halfwidth: float32 [1], replicated, may hold values from 0.8 to 1.6
Outputs:
- rotated: float32 [128, 4096], P('states', 'nodes')
The draws below stay inside these ranges and needn't reach their ends.
Inputs may be any that keep to these rules, and one draw needn't show every extreme that they name: `offsets`: the first entry of every row is 0; the values -4 and 4 occur in every draw.
All inputs are finite; a program needn't handle non-finite values.
Results may differ from the reference program's by a relative error of at most 0.0003.
Values may be sent and summed in bfloat16 or wider, within the bound.
No kernel may reach another device: no remote copies, remote signals or barrier semaphores. Data moves between devices by JAX's collectives and lax.ppermute only.
A program may use at most 64 MiB of HBM per device.

```python
import jax
import jax.numpy as jnp
from jax import lax

BLOCK = 64
NEIGH = 27
REACH = 4
STATES = 128
NODES = 4096
BLOCKS = 64
N_NODES = 8


def draw_offsets(key, part):
    key = jax.random.fold_in(key, 7)
    key_one, key_two = jax.random.split(key, 2)
    values = jax.random.randint(key_one, (BLOCKS, NEIGH), -REACH, REACH + 1)
    values = values.at[:, 0].set(0)
    picked = jax.random.randint(key_two, (2,), 0, BLOCKS)
    values = values.at[picked[0], 1].set(-REACH)
    values = values.at[picked[1], 2].set(REACH)
    return values.astype(jnp.int32)


def block_levels(stream_key, shape, cuts, low, high):
    gain, own = 1.0, jax.random.fold_in(stream_key, 6)
    for dim, shards_of in cuts:
        steps = jnp.exp(jax.random.uniform(jax.random.fold_in(own, dim), (shards_of,), jnp.float32, low / len(cuts), high / len(cuts)))
        gain = gain * jnp.repeat(steps, shape[dim] // shards_of).reshape([-1 if axis == dim else 1 for axis in range(len(shape))])
    return gain


def bell_draw(rng, extent, scale, bound, pieces=(), kind=jnp.bfloat16):
    values = jax.random.normal(rng, extent, jnp.float32) * scale
    if len(pieces) > 0:
        values = block_levels(rng, extent, pieces, -0.22, 0.18) * values
    return jnp.clip(values, min=-bound, max=bound).astype(kind)


def setup_inputs(seed: int = 0) -> dict:
    splits = jax.random.split(jax.random.key(seed), 6)
    return {
        "states_block": bell_draw(splits[0], (STATES, NODES), 1.0, 6.0, ((0, 4), (1, 8)), jnp.float32),
        "hamiltonian": bell_draw(splits[1], (BLOCKS, BLOCK, NEIGH * BLOCK), (NEIGH * BLOCK) ** -0.5, 0.15625, ((0, 8),)),
        "offsets": draw_offsets(jax.random.fold_in(splits[5], 71), 0),
        "center": jnp.clip(jax.random.uniform(splits[3], (1,), jnp.float32, -0.5, 0.5), -0.5, 0.5),
        "halfwidth": jnp.clip(jax.random.uniform(splits[4], (1,), jnp.float32, 0.8, 1.6), 0.8, 1.6),
    }


def apply_operator(field, hamiltonian, offsets):
    group = BLOCKS // N_NODES
    blocked = field.reshape(STATES, BLOCKS, BLOCK)
    ham_groups = hamiltonian.reshape(BLOCKS // group, group, BLOCK, NEIGH * BLOCK)
    off_groups = offsets.reshape(BLOCKS // group, group, NEIGH)
    starts = (jnp.arange(BLOCKS // group) * group).astype(jnp.int32)

    def one_group(items):
        ham_part, off_part, first = items
        index = (first + jnp.arange(group, dtype=jnp.int32)[:, None] + off_part) % BLOCKS
        picked = blocked[:, index].reshape(STATES, group, NEIGH * BLOCK)
        return jnp.einsum('bim,cbm->cbi', ham_part.astype(jnp.float32), picked, precision=lax.Precision.HIGHEST)
    result = lax.map(one_group, (ham_groups, off_groups, starts))
    return jnp.transpose(result, (1, 0, 2, 3)).reshape(STATES, NODES)

def reference(states_block, hamiltonian, offsets, center, halfwidth):
    shift = center[0]
    width = halfwidth[0]
    first = (apply_operator(states_block, hamiltonian, offsets) - shift * states_block) / width
    second = 2.0 * (apply_operator(first, hamiltonian, offsets) - shift * first) / width - states_block
    intersection = jnp.dot(second, second.T, precision=lax.Precision.HIGHEST) / NODES
    lower = jnp.linalg.cholesky(intersection)
    inverse = lax.linalg.triangular_solve(lower, jnp.eye(STATES, dtype=jnp.float32), left_side=True, lower=True)
    return jnp.dot(inverse, second, precision=lax.Precision.HIGHEST)
```

```python
import functools

import jax
import jax.numpy as jnp
from jax import lax
from jax.experimental import pallas as pl
from jax.experimental.pallas import tpu as pltpu
from jax.sharding import PartitionSpec as P

REACH = 4
LANES = 128
PANEL = 16
VMEM = pl.BlockSpec(memory_space=pltpu.VMEM)
SMEM = pl.BlockSpec(memory_space=pltpu.SMEM)
NT = (((1,), (1,)), ((), ()))
TN = (((0,), (0,)), ((), ()))


def halves(x):
    high = x.astype(jnp.bfloat16)
    return high, (x - high.astype(jnp.float32)).astype(jnp.bfloat16)


def stacked(x):
    return jnp.concatenate(halves(x), axis=0)


def apply_operator(left, own, right, hamiltonian, offsets, pairs):
    rows = own.shape[0]
    count, size, depth = hamiltonian.shape
    neighbours = depth // size
    line = stacked(jnp.concatenate([left, own, right], axis=1))
    blocks = line.shape[1] // size
    for tile in range(blocks // 2):
        pairs[2 * tile + 1] = line[:, tile * LANES : (tile + 1) * LANES]
    for tile in range(blocks // 2 + 1):
        lo, hi = tile * LANES - size, tile * LANES + size
        if lo < 0:
            part = jnp.concatenate([line[:, :size], line[:, :size]], axis=1)
        elif hi > line.shape[1]:
            part = jnp.concatenate([line[:, lo:], line[:, lo:]], axis=1)
        else:
            part = line[:, lo:hi]
        pairs[2 * tile] = part
    low_lanes = lax.broadcasted_iota(jnp.int32, (2 * rows, LANES), 1) < size
    results = []
    for b in range(count):
        picked = []
        for k in range(0, neighbours - 1, 2):
            first = pairs[b + REACH + offsets[b, k] + 1]
            second = pairs[b + REACH + offsets[b, k + 1]]
            picked.append(jnp.where(low_lanes, first, second))
        whole = len(picked) * LANES
        total = lax.dot_general(
            jnp.concatenate(picked, axis=1),
            hamiltonian[b, :, :whole],
            NT,
            preferred_element_type=jnp.float32,
        )
        if neighbours % 2:
            last = pairs[b + REACH + offsets[b, neighbours - 1] + 1][:, :size]
            total += lax.dot_general(
                last, hamiltonian[b, :, whole:], NT, preferred_element_type=jnp.float32
            )
        results.append(total[:rows] + total[rows:])
    return jnp.concatenate(results, axis=1)


def first_kernel(left, own, right, hamiltonian, offsets, center, width, out, head, tail, pairs):
    rim = head.shape[1]
    field = own[...]
    applied = apply_operator(left[:, -rim:], field, right[:, :rim], hamiltonian, offsets, pairs)
    first = (applied - center[0] * field) / width[0]
    out[...] = first
    head[...] = first[:, :rim]
    tail[...] = first[:, -rim:]


def second_kernel(left, own, right, hamiltonian, offsets, center, width, before, out, pairs):
    field = own[...]
    applied = apply_operator(left[...], field, right[...], hamiltonian, offsets, pairs)
    out[...] = 2.0 * (applied - center[0] * field) / width[0] - before[...]


def gram_kernel(total_nodes, *refs):
    parts, (gathered, gram) = refs[:-2], refs[-2:]
    count = len(parts)
    rows = parts[0].shape[0]
    me = lax.axis_index("states")
    for step, part in enumerate(parts):
        place = lax.rem(me + count - step, count)
        high, low = halves(part[...])
        gathered[0, pl.ds(pl.multiple_of(place * rows, rows), rows)] = high
        gathered[1, pl.ds(pl.multiple_of(place * rows, rows), rows)] = low
    states = count * rows
    both = gathered[...].reshape(2 * states, -1)
    terms = lax.dot_general(both, both, NT, preferred_element_type=jnp.float32)
    gram[...] = (terms[:states, :states] + (terms[:states, states:] + terms[states:, :states])) * (
        1.0 / total_nodes
    )


def inverse_factor(matrix, inverse):
    order = matrix.shape[0]
    lane = lax.broadcasted_iota(jnp.int32, (PANEL, order), 1)
    row = lax.broadcasted_iota(jnp.int32, (PANEL, order), 0)
    for start in range(0, order, PANEL):
        stop = start + PANEL
        panel = matrix[start:stop]
        inside = (lane >= start) & (lane < stop)
        columns = [
            jnp.broadcast_to(panel[:, start + k : start + k + 1], (PANEL, order))
            for k in range(PANEL)
        ]
        rows = jnp.where(inside, jnp.where(lane == row + start, 1.0, 0.0), panel)
        for j in range(PANEL):
            scale = lax.rsqrt(columns[j][j : j + 1])
            factor = columns[j] * scale
            pivot = rows[j : j + 1] * scale
            rows = jnp.where(row > j, rows - factor * pivot, jnp.where(row == j, pivot, rows))
            for k in range(j + 1, PANEL):
                columns[k] = columns[k] - factor * (columns[k][j : j + 1] * scale)
        inverse[start:stop] = jnp.where(lane < stop, rows, 0.0)
        if stop < order:
            beyond = jnp.where(lane >= stop, rows, 0.0)
            update = lax.dot_general(
                beyond, rows, TN, precision=lax.Precision.HIGHEST, preferred_element_type=jnp.float32
            )
            rest = matrix[stop:]
            rest_lane = lax.broadcasted_iota(jnp.int32, rest.shape, 1)
            kept = jnp.where((rest_lane >= start) & (rest_lane < stop), 0.0, rest)
            matrix[stop:] = kept - update[stop:]


def rotate_kernel(grams, gathered, out, matrix, inverse):
    total = grams[0]
    for i in range(1, grams.shape[0]):
        total += grams[i]
    matrix[...] = total
    inverse_factor(matrix, inverse)
    rows = out.shape[0]
    me = lax.axis_index("states")
    high, low = halves(inverse[pl.ds(pl.multiple_of(me * rows, rows), rows)])
    both = lax.dot_general(
        jnp.concatenate([high, low], axis=0),
        gathered[0],
        (((1,), (0,)), ((), ())),
        preferred_element_type=jnp.float32,
    )
    rest = jnp.dot(high, gathered[1], preferred_element_type=jnp.float32)
    out[...] = both[:rows] + (both[rows:] + rest)


def on_device(states_block, hamiltonian, offsets, center, halfwidth):
    rows, local = states_block.shape
    count, size, depth = hamiltonian.shape
    rim = REACH * size
    ring = lax.axis_size("nodes")
    parts = lax.axis_size("states")
    states = rows * parts
    up = [(i, (i + 1) % ring) for i in range(ring)]
    down = [((i + 1) % ring, i) for i in range(ring)]
    f32 = jnp.float32

    def shape(*dims, dtype=f32):
        return jax.ShapeDtypeStruct(dims, dtype)

    pairs = pltpu.VMEM((count + 2 * REACH + 1, 2 * rows, LANES), jnp.bfloat16)
    from_left = lax.ppermute(states_block, "nodes", up)
    from_right = lax.ppermute(states_block, "nodes", down)
    first, head, tail = pl.pallas_call(
        first_kernel,
        out_shape=(shape(rows, local), shape(rows, rim), shape(rows, rim)),
        in_specs=[VMEM] * 4 + [SMEM] * 3,
        out_specs=(VMEM,) * 3,
        scratch_shapes=[pairs],
        name="first",
    )(from_left, states_block, from_right, hamiltonian, offsets, center, halfwidth)
    from_left = lax.ppermute(tail, "nodes", up)
    from_right = lax.ppermute(head, "nodes", down)
    second = pl.pallas_call(
        second_kernel,
        out_shape=shape(rows, local),
        in_specs=[VMEM] * 4 + [SMEM] * 3 + [VMEM],
        out_specs=VMEM,
        scratch_shapes=[pairs],
        name="second",
    )(from_left, first, from_right, hamiltonian, offsets, center, halfwidth, states_block)
    gathering = [second] + [
        lax.ppermute(second, "states", [(i, (i + k) % parts) for i in range(parts)])
        for k in range(1, parts)
    ]
    gathered, gram = pl.pallas_call(
        functools.partial(gram_kernel, local * ring),
        out_shape=(shape(2, states, local, dtype=jnp.bfloat16), shape(states, states)),
        in_specs=[VMEM] * parts,
        out_specs=(VMEM, VMEM),
        name="gram",
    )(*gathering)
    if ring <= 16:
        grams = lax.all_gather(gram, "nodes")
    else:
        grams = lax.psum(gram, "nodes")[None]
    return pl.pallas_call(
        rotate_kernel,
        out_shape=shape(rows, local),
        in_specs=[VMEM] * 2,
        out_specs=VMEM,
        scratch_shapes=[pltpu.VMEM((states, states), f32)] * 2,
        name="rotate",
    )(grams, gathered)


def solution(mesh):
    placed = (P("states", "nodes"), P("nodes", None, None), P("nodes", None), P(), P())
    return jax.shard_map(
        on_device, mesh=mesh, in_specs=placed, out_specs=P("states", "nodes"), check_vma=False
    )
```

```python
import functools

import jax
import jax.numpy as jnp
from jax import lax
from jax.experimental import pallas as pl
from jax.experimental.pallas import tpu as pltpu
from jax.sharding import PartitionSpec as P

REACH = 4
LANES = 128
PANEL = 16
VMEM = pl.BlockSpec(memory_space=pltpu.VMEM)
SMEM = pl.BlockSpec(memory_space=pltpu.SMEM)
HBM = pl.BlockSpec(memory_space=pltpu.HBM)
ROOM = pltpu.CompilerParams(vmem_limit_bytes=16 * 2**20)
NT = (((1,), (1,)), ((), ()))
TN = (((0,), (0,)), ((), ()))


def halves(x):
    high = x.astype(jnp.bfloat16)
    return high, (x - high.astype(jnp.float32)).astype(jnp.bfloat16)


def stacked(x):
    return jnp.concatenate(halves(x), axis=0)


def swapped(tile):
    half = LANES // 2
    return jnp.concatenate([tile[:, half:], tile[:, :half]], axis=1)


def prepare(there, offsets_there, *refs):
    near_band, far_band, matrix, near_sums, far_sums, offsets, sems = refs
    odd = lax.axis_index("nodes") % 2 == 1
    count, size, depth = matrix.shape
    neighbours = depth // size
    span = 2 * REACH + 1
    begin = jnp.where(odd, 0, count - REACH)

    def copy(b):
        return pltpu.make_async_copy(there.at[b], matrix.at[b], sems.at[b])

    distances = pltpu.make_async_copy(offsets_there, offsets, sems.at[count])
    distances.start()
    rows = [lax.rem(begin + r, count) for r in range(count)]
    for b in rows:
        copy(b).start()
    low_lanes = lax.broadcasted_iota(jnp.int32, (size, LANES), 1) < size
    for sums in (near_sums, far_sums):
        sums[...] = jnp.zeros(sums.shape, jnp.float32)
    distances.wait()
    for sums, band, mine in ((near_sums, near_band, rows[:REACH]), (far_sums, far_band, rows[REACH:])):
        for b in mine:
            copy(b).wait()
        for k in range(0, neighbours, 2):
            for r, b in enumerate(mine):
                tile = matrix[b, :, k * size : min(k + 2, neighbours) * size].astype(jnp.float32)
                if tile.shape[1] < LANES:
                    tile = jnp.concatenate([tile, jnp.zeros_like(tile)], axis=1)
                for j in range(k, min(k + 2, neighbours)):
                    place = offsets[b, j] + REACH
                    sums[r, j - k, place] = sums[r, j - k, place] + tile
        for r in range(REACH):
            for t in range(3 * REACH // 2):
                low, high = 2 * t - r, 2 * t + 1 - r
                zero = jnp.zeros((size, LANES), jnp.float32)
                even_low, odd_low = (
                    (sums[r, 0, low], sums[r, 1, low]) if 0 <= low < span else (zero, zero)
                )
                even_high, odd_high = (
                    (sums[r, 0, high], sums[r, 1, high]) if 0 <= high < span else (zero, zero)
                )
                whole = jnp.where(low_lanes, even_low, odd_high) + swapped(
                    jnp.where(low_lanes, even_high, odd_low)
                )
                top, rest = halves(whole)
                place = (slice(r * size, (r + 1) * size), slice(t * LANES, (t + 1) * LANES))
                band[(0, *place)] = top
                band[(1, *place)] = rest


def side(field, before):
    half = field.shape[1] // 2
    return jnp.where(before, field[:, :half], field[:, half:])


def joined(near, far, odd):
    return jnp.concatenate([jnp.where(odd, near, far), jnp.where(odd, far, near)], axis=1)


def before_own(is_near):
    odd = lax.axis_index("nodes") % 2
    return odd == (1 if is_near else 0)


def window(own, rim, before):
    wide = rim.shape[1]
    return jnp.concatenate(
        [
            jnp.where(before, rim, own[:, :wide]),
            jnp.where(before, own[:, :wide], own[:, wide:]),
            jnp.where(before, own[:, wide:], rim),
        ],
        axis=1,
    )


def apply_band(field, band):
    rows = field.shape[0]
    field = stacked(field)
    both = lax.dot_general(field, band[0], NT, preferred_element_type=jnp.float32)
    rest = lax.dot_general(field[:rows], band[1], NT, preferred_element_type=jnp.float32)
    return both[:rows] + (both[rows:] + rest)


def first_kernel(is_near, rim, own, band, out):
    before = before_own(is_near)
    out[...] = apply_band(window(own[...], side(rim[...], jnp.logical_not(before)), before), band)


def second_half(is_near, rim, near, far, band, earlier_rim, earlier, center, width):
    before = before_own(is_near)
    shift, scale = center[0], 1.0 / width[0]
    applied = window(joined(near[...], far[...], before_own(True)), rim[...], before)
    field = earlier[...]
    states = window(field, side(earlier_rim[...], jnp.logical_not(before)), before)
    first = (applied - shift * states) * scale
    half = rim.shape[1]
    mine = first[:, half : 2 * half]
    return 2.0 * ((apply_band(first, band) - shift * mine) * scale) - side(field, before)


def second_near(*refs):
    refs[-1][...] = second_half(True, *refs[:-1])


def second_far(*refs):
    *rest, done, out = refs
    out[...] = joined(done[...], second_half(False, *rest), before_own(True))


def gram_kernel(total_nodes, steps, *refs):
    parts, (gathered, gram) = refs[:-2], refs[-2:]
    rows = parts[0].shape[0]
    me = lax.axis_index("states")
    for step, part in zip(steps, parts, strict=True):
        place = pl.ds(pl.multiple_of((me ^ step) * rows, rows), rows)
        high, low = halves(part[...])
        gathered[0, place] = high
        gathered[1, place] = low
    states = len(parts) * rows
    both = gathered[...].reshape(2 * states, -1)
    terms = lax.dot_general(both, both, NT, preferred_element_type=jnp.float32)
    gram[...] = (terms[:states, :states] + (terms[:states, states:] + terms[states:, :states])) * (
        1.0 / total_nodes
    )


def sum_kernel(*refs):
    refs[-1][...] = functools.reduce(jnp.add, [ref[...] for ref in refs[:-1]])


def inverse_factor(matrix, inverse):
    order = matrix.shape[0]
    lane = lax.broadcasted_iota(jnp.int32, (PANEL, order), 1)
    row = lax.broadcasted_iota(jnp.int32, (PANEL, order), 0)
    for start in range(0, order, PANEL):
        stop = start + PANEL
        panel = matrix[start:stop]
        inside = (lane >= start) & (lane < stop)
        columns = [
            jnp.broadcast_to(panel[:, start + k : start + k + 1], (PANEL, order))
            for k in range(PANEL)
        ]
        rows = jnp.where(inside, jnp.where(lane == row + start, 1.0, 0.0), panel)
        for j in range(PANEL):
            scale = lax.rsqrt(columns[j][j : j + 1])
            factor = columns[j] * scale
            pivot = rows[j : j + 1] * scale
            rows = jnp.where(row > j, rows - factor * pivot, jnp.where(row == j, pivot, rows))
            for k in range(j + 1, PANEL):
                columns[k] = columns[k] - factor * (columns[k][j : j + 1] * scale)
        inverse[start:stop] = jnp.where(lane < stop, rows, 0.0)
        if stop < order:
            beyond = jnp.where(lane >= stop, rows, 0.0)
            update = lax.dot_general(
                beyond, rows, TN, precision=lax.Precision.HIGHEST, preferred_element_type=jnp.float32
            )
            rest = matrix[stop:]
            rest_lane = lax.broadcasted_iota(jnp.int32, rest.shape, 1)
            kept = jnp.where((rest_lane >= start) & (rest_lane < stop), 0.0, rest)
            matrix[stop:] = kept - update[stop:]


def rotate_kernel(*refs):
    *grams, gathered, out, matrix, inverse = refs
    matrix[...] = functools.reduce(jnp.add, [gram[...] for gram in grams])
    inverse_factor(matrix, inverse)
    rows = out.shape[0]
    me = lax.axis_index("states")
    high, low = halves(inverse[pl.ds(pl.multiple_of(me * rows, rows), rows)])
    both = lax.dot_general(
        jnp.concatenate([high, low], axis=0),
        gathered[0],
        (((1,), (0,)), ((), ())),
        preferred_element_type=jnp.float32,
    )
    rest = jnp.dot(high, gathered[1], preferred_element_type=jnp.float32)
    out[...] = both[:rows] + (both[rows:] + rest)


def near(x):
    return pltpu.with_memory_space_constraint(x, pltpu.VMEM)


def exchange(x, axis, step):
    count = lax.axis_size(axis)
    return near(lax.ppermute(x, axis, [(i, i ^ step) for i in range(count)]))


def on_device(states_block, hamiltonian, offsets, center, halfwidth):
    rows, local = states_block.shape
    count, size, depth = hamiltonian.shape
    half = local // 2
    ring = lax.axis_size("nodes")
    parts = lax.axis_size("states")
    states = rows * parts
    off_chip = [(i, (i + 1 if i % 2 else i - 1) % ring) for i in range(ring)]
    f32, bf16 = jnp.float32, jnp.bfloat16
    field = pltpu.VMEM((rows, local), f32)
    part = pltpu.VMEM((rows, half), f32)
    square = pltpu.VMEM((states, states), f32)
    band = pltpu.VMEM((2, REACH * size, 3 * REACH * size), bf16)
    sums = pltpu.VMEM((REACH, 2, 2 * REACH + 1, size, LANES), f32)

    def over_links(x):
        return near(lax.ppermute(x, "nodes", off_chip))

    def call(kernel, out, *operands, name):
        return near(
            pl.pallas_call(
                kernel,
                out_shape=out,
                in_specs=[SMEM if x.size == 1 else VMEM for x in operands],
                out_specs=VMEM,
                compiler_params=ROOM,
                name=name,
            )(*operands)
        )

    far_states = over_links(states_block)
    near_states = exchange(states_block, "nodes", 1)
    near_band, far_band = pl.pallas_call(
        prepare,
        out_shape=(band, band),
        in_specs=[HBM, HBM],
        out_specs=(VMEM, VMEM),
        scratch_shapes=[
            pltpu.VMEM(hamiltonian.shape, bf16),
            sums,
            sums,
            pltpu.SMEM(offsets.shape, jnp.int32),
            pltpu.SemaphoreType.DMA((count + 1,)),
        ],
        compiler_params=ROOM,
        name="prepare",
    )(*(pltpu.with_memory_space_constraint(x, pltpu.HBM) for x in (hamiltonian, offsets)))
    near_band, far_band = near(near_band), near(far_band)
    own = near(states_block)
    near_part = call(
        functools.partial(first_kernel, True), part, near_states, own, near_band, name="first_near"
    )
    near_rim = exchange(near_part, "nodes", 1)
    far_part = call(
        functools.partial(first_kernel, False), part, far_states, own, far_band, name="first_far"
    )
    far_rim = over_links(far_part)
    parts_of = (near_part, far_part)
    scalars = (center, halfwidth)
    near_second = call(
        second_near, part, near_rim, *parts_of, near_band, near_states, own, *scalars, name="second_near"
    )
    second = call(
        second_far,
        field,
        far_rim,
        *parts_of,
        far_band,
        far_states,
        own,
        *scalars,
        near_second,
        name="second_far",
    )
    steps = sorted(range(1, parts), key=lambda k: (k % 2, k))
    gathering = [second] + [exchange(second, "states", k) for k in steps]
    gathered, gram = pl.pallas_call(
        functools.partial(gram_kernel, local * ring, [0] + steps),
        out_shape=(pltpu.VMEM((2, states, local), bf16), square),
        in_specs=[VMEM] * parts,
        out_specs=(VMEM, VMEM),
        compiler_params=ROOM,
        name="gram",
    )(*gathering)
    terms = [near(gram), exchange(near(gram), "nodes", 1)]
    bit = 2
    while bit < ring:
        total = near(
            pl.pallas_call(
                sum_kernel,
                out_shape=square,
                in_specs=[VMEM] * len(terms),
                out_specs=VMEM,
                compiler_params=ROOM,
                name="sum",
            )(*terms)
        )
        peers = [bit, 2 * bit, 3 * bit] if 2 * bit < ring else [bit]
        terms = [total] + [exchange(total, "nodes", k) for k in peers]
        bit *= 4
    return pl.pallas_call(
        rotate_kernel,
        out_shape=jax.ShapeDtypeStruct((rows, local), f32),
        in_specs=[VMEM] * (len(terms) + 1),
        out_specs=VMEM,
        scratch_shapes=[square, square],
        compiler_params=ROOM,
        name="rotate",
    )(*terms, near(gathered))


def solution(mesh):
    placed = (P("states", "nodes"), P("nodes", None, None), P("nodes", None), P(), P())
    return jax.shard_map(
        on_device, mesh=mesh, in_specs=placed, out_specs=P("states", "nodes"), check_vma=False
    )
```

```python
import functools

import jax
import jax.numpy as jnp
from jax import lax
from jax.experimental import pallas as pl
from jax.experimental.pallas import tpu as pltpu
from jax.sharding import PartitionSpec as P

REACH = 4
LANES = 128
PANEL = 32
STEP = 16
VMEM = pl.BlockSpec(memory_space=pltpu.VMEM)
SMEM = pl.BlockSpec(memory_space=pltpu.SMEM)
HBM = pl.BlockSpec(memory_space=pltpu.HBM)
ROOM = pltpu.CompilerParams(vmem_limit_bytes=16 * 2**20)
NT = (((1,), (1,)), ((), ()))
TN = (((0,), (0,)), ((), ()))


def halves(x):
    high = x.astype(jnp.bfloat16)
    return high, (x - high.astype(jnp.float32)).astype(jnp.bfloat16)


def stacked(x):
    return jnp.concatenate(halves(x), axis=0)


def swapped(tile):
    half = LANES // 2
    return jnp.concatenate([tile[:, half:], tile[:, :half]], axis=1)


def prepare(there, offsets_there, near_band, far_band, blocks, offsets, sems, *sums):
    count = there.shape[0]
    rows = half_rows(True, count) + half_rows(False, count)
    copies = [pltpu.make_async_copy(offsets_there, offsets, sems.at[count])]
    copies += [
        pltpu.make_async_copy(there.at[b], blocks.at[r], sems.at[r]) for r, b in enumerate(rows)
    ]
    for copy in copies:
        copy.start()
    for one in sums:
        one[...] = jnp.zeros(one.shape, jnp.float32)
    for copy in copies:
        copy.wait()
    add_up(blocks, rows, offsets, sums)
    make_band(sums[:REACH], near_band)
    make_band(sums[REACH:], far_band)


def half_rows(is_near, count):
    begin = jnp.where(before_own(is_near), 0, count - REACH)
    return [begin + r for r in range(REACH)]


def add_up(blocks, rows, offsets, sums):
    _, size, depth = blocks.shape
    neighbours = depth // size
    half = size // 2
    low_lanes = lax.broadcasted_iota(jnp.int32, (half, LANES), 1) < size
    for k in range(0, neighbours, 2):
        for r, (b, one) in enumerate(zip(rows, sums, strict=True)):
            tile = blocks[r, :, k * size : min(k + 2, neighbours) * size]
            if tile.shape[1] < LANES:
                tile = jnp.concatenate([tile, jnp.zeros_like(tile)], axis=1)
            turned = swapped(tile).astype(jnp.float32)
            tile = tile.astype(jnp.float32)
            place = offsets[b, k] + REACH
            one[place] = one[place] + jnp.where(low_lanes, tile[:half], turned[half:])
            if k + 1 < neighbours:
                place = offsets[b, k + 1] + REACH
                one[place] = one[place] + jnp.where(low_lanes, turned[:half], tile[half:])


def make_band(sums, band):
    span, half, _ = sums[0].shape
    size = 2 * half
    low_lanes = lax.broadcasted_iota(jnp.int32, (half, LANES), 1) < size
    zero = jnp.zeros((half, LANES), jnp.float32)
    for r, one in enumerate(sums):
        folded = [one[p] for p in range(span)]
        turned = [swapped(x) for x in folded]
        for t in range(3 * REACH // 2):
            low, high = 2 * t - r, 2 * t + 1 - r
            even, even_turned = (folded[low], turned[low]) if 0 <= low < span else (zero, zero)
            odd, odd_turned = (folded[high], turned[high]) if 0 <= high < span else (zero, zero)
            whole = jnp.concatenate(
                [jnp.where(low_lanes, even, odd_turned), jnp.where(low_lanes, even_turned, odd)], axis=0
            )
            top, rest = halves(whole)
            place = (slice(r * size, (r + 1) * size), slice(t * LANES, (t + 1) * LANES))
            band[(0, *place)] = top
            band[(1, *place)] = rest


def side(field, before):
    half = field.shape[1] // 2
    return jnp.where(before, field[:, :half], field[:, half:])


def joined(near, far, odd):
    return jnp.concatenate([jnp.where(odd, near, far), jnp.where(odd, far, near)], axis=1)


def before_own(is_near):
    odd = lax.axis_index("nodes") % 2
    return odd == (1 if is_near else 0)


def window(own, rim, before):
    wide = rim.shape[1]
    return jnp.concatenate(
        [
            jnp.where(before, rim, own[:, :wide]),
            jnp.where(before, own[:, :wide], own[:, wide:]),
            jnp.where(before, own[:, wide:], rim),
        ],
        axis=1,
    )


def apply_band(field, band):
    rows = field.shape[0]
    field = stacked(field)
    both = lax.dot_general(field, band[0], NT, preferred_element_type=jnp.float32)
    rest = lax.dot_general(field[:rows], band[1], NT, preferred_element_type=jnp.float32)
    return both[:rows] + (both[rows:] + rest)


def first_half(is_near, rim, own, band):
    before = before_own(is_near)
    return apply_band(window(own[...], side(rim[...], jnp.logical_not(before)), before), band)


def first_near(rim, own, band, out):
    out[...] = first_half(True, rim, own, band)


def first_far(rim, own, band, out):
    out[...] = first_half(False, rim, own, band)


def second_half(is_near, rim, near, far, band, earlier_rim, earlier, center, width):
    before = before_own(is_near)
    shift, scale = center[0], 1.0 / width[0]
    applied = window(joined(near[...], far[...], before_own(True)), rim[...], before)
    field = earlier[...]
    states = window(field, side(earlier_rim[...], jnp.logical_not(before)), before)
    first = (applied - shift * states) * scale
    half = rim.shape[1]
    mine = first[:, half : 2 * half]
    return 2.0 * ((apply_band(first, band) - shift * mine) * scale) - side(field, before)


def second_near(*refs):
    refs[-1][...] = second_half(True, *refs[:-1])


def second_far(*refs):
    *rest, done, out = refs
    out[...] = joined(done[...], second_half(False, *rest), before_own(True))


def gram_kernel(total_nodes, steps, *refs):
    parts, (gathered, gram) = refs[:-2], refs[-2:]
    rows = parts[0].shape[0]
    me = lax.axis_index("states")
    for step, part in zip(steps, parts, strict=True):
        place = pl.ds(pl.multiple_of((me ^ step) * rows, rows), rows)
        high, low = halves(part[...])
        gathered[0, place] = high
        gathered[1, place] = low
    states = len(parts) * rows
    both = gathered[...].reshape(2 * states, -1)
    terms = lax.dot_general(both, both, NT, preferred_element_type=jnp.float32)
    gram[...] = (terms[:states, :states] + (terms[:states, states:] + terms[states:, :states])) * (
        1.0 / total_nodes
    )


def sum_kernel(*refs):
    refs[-1][...] = functools.reduce(jnp.add, [ref[...] for ref in refs[:-1]])


def thirds(x):
    high = x.astype(jnp.bfloat16)
    rest = x - high.astype(jnp.float32)
    middle = rest.astype(jnp.bfloat16)
    return high, middle, (rest - middle.astype(jnp.float32)).astype(jnp.bfloat16)


def outer(left, right):
    a, b, c = thirds(left)
    d, e, f = thirds(right)
    return lax.dot_general(
        jnp.concatenate([a, a, b, a, b, c], axis=0),
        jnp.concatenate([d, e, d, f, e, d], axis=0),
        TN,
        preferred_element_type=jnp.float32,
    )


def inverse_factor(matrix, inverse):
    order = matrix.shape[0]
    lane = lax.broadcasted_iota(jnp.int32, (8, order), 1)
    sub = lax.broadcasted_iota(jnp.int32, (8, order), 0)
    for start in range(0, order, PANEL):
        stop = start + PANEL
        groups = [matrix[i : i + 8] for i in range(start, stop, 8)]
        done = []
        for first in range(start, stop, STEP):
            after = first + STEP
            inside = (lane >= first) & (lane < after)
            columns = [
                [jnp.broadcast_to(g[:, k : k + 1], g.shape) for g in groups]
                for k in range(first, after)
            ]
            for i, g in enumerate(groups):
                unit = jnp.where(lane == sub + (first + 8 * i), 1.0, 0.0) if 8 * i < STEP else 0.0
                groups[i] = jnp.where(inside, unit, g)
            for j in range(STEP):
                own, s = divmod(j, 8)
                scale = lax.rsqrt(columns[j][own][s : s + 1])
                pivot = groups[own][s : s + 1] * scale
                heads = [column[own][s : s + 1] * scale for column in columns]
                for i in range(own, len(groups)):
                    factor = columns[j][i] * scale
                    less = groups[i] - factor * pivot
                    if i == own:
                        less = jnp.where(sub > s, less, jnp.where(sub == s, pivot, groups[i]))
                    groups[i] = less
                    if i > own or s < 7:
                        for k in range(j + 1, STEP):
                            columns[k][i] = columns[k][i] - factor * heads[k]
            beyond = (lane >= after) & (lane < stop)
            done += [jnp.where(beyond, 0.0, g) for g in groups[: STEP // 8]]
            groups = groups[STEP // 8 :]
        rows = jnp.concatenate(done, axis=0)
        right = lax.broadcasted_iota(jnp.int32, rows.shape, 1) >= stop
        inverse[start:stop] = jnp.where(right, 0.0, rows)
        if stop < order:
            update = outer(jnp.where(right, rows, 0.0), rows)
            rest = matrix[stop:]
            at = lax.broadcasted_iota(jnp.int32, rest.shape, 1)
            kept = jnp.where((at >= start) & (at < stop), 0.0, rest)
            matrix[stop:] = kept - update[stop:]


def rotate_kernel(*refs):
    *grams, gathered, out, matrix, inverse = refs
    matrix[...] = functools.reduce(jnp.add, [gram[...] for gram in grams])
    inverse_factor(matrix, inverse)
    rows = out.shape[0]
    me = lax.axis_index("states")
    high, low = halves(inverse[pl.ds(pl.multiple_of(me * rows, rows), rows)])
    both = lax.dot_general(
        jnp.concatenate([high, low], axis=0),
        gathered[0],
        (((1,), (0,)), ((), ())),
        preferred_element_type=jnp.float32,
    )
    rest = jnp.dot(high, gathered[1], preferred_element_type=jnp.float32)
    out[...] = both[:rows] + (both[rows:] + rest)


def near(x):
    return pltpu.with_memory_space_constraint(x, pltpu.VMEM)


def there(x):
    return pltpu.with_memory_space_constraint(x, pltpu.HBM)


def exchange(x, axis, step):
    count = lax.axis_size(axis)
    return near(lax.ppermute(x, axis, [(i, i ^ step) for i in range(count)]))


def on_device(states_block, hamiltonian, offsets, center, halfwidth):
    rows, local = states_block.shape
    count, size, depth = hamiltonian.shape
    half = local // 2
    ring = lax.axis_size("nodes")
    parts = lax.axis_size("states")
    states = rows * parts
    off_chip = [(i, (i + 1 if i % 2 else i - 1) % ring) for i in range(ring)]
    f32, bf16 = jnp.float32, jnp.bfloat16
    field = pltpu.VMEM((rows, local), f32)
    part = pltpu.VMEM((rows, half), f32)
    square = pltpu.VMEM((states, states), f32)
    band = pltpu.VMEM((2, REACH * size, 3 * REACH * size), bf16)
    sums = pltpu.VMEM((2 * REACH + 1, size // 2, LANES), f32)

    def over_links(x):
        return near(lax.ppermute(x, "nodes", off_chip))

    def call(kernel, out, *operands, name):
        return near(
            pl.pallas_call(
                kernel,
                out_shape=out,
                in_specs=[SMEM if x.size == 1 else VMEM for x in operands],
                out_specs=VMEM,
                compiler_params=ROOM,
                name=name,
            )(*operands)
        )

    far_states = over_links(states_block)
    near_states = exchange(states_block, "nodes", 1)
    near_band, far_band = pl.pallas_call(
        prepare,
        out_shape=(band, band),
        in_specs=[HBM, HBM],
        out_specs=(VMEM, VMEM),
        scratch_shapes=[
            pltpu.VMEM(hamiltonian.shape, bf16),
            pltpu.SMEM(offsets.shape, jnp.int32),
            pltpu.SemaphoreType.DMA((count + 1,)),
            *[sums] * count,
        ],
        compiler_params=ROOM,
        name="prepare",
    )(there(hamiltonian), there(offsets))
    near_band, far_band = near(near_band), near(far_band)
    own = near(states_block)
    near_part = call(first_near, part, near_states, own, near_band, name="first_near")
    near_rim = exchange(near_part, "nodes", 1)
    far_part = call(first_far, part, far_states, own, far_band, name="first_far")
    far_rim = over_links(far_part)
    parts_of = (near_part, far_part)
    scalars = (center, halfwidth)
    near_second = call(
        second_near, part, near_rim, *parts_of, near_band, near_states, own, *scalars, name="second_near"
    )
    second = call(
        second_far,
        field,
        far_rim,
        *parts_of,
        far_band,
        far_states,
        own,
        *scalars,
        near_second,
        name="second_far",
    )
    steps = sorted(range(1, parts), key=lambda k: (k % 2, k))
    gathering = [second] + [exchange(second, "states", k) for k in steps]
    gathered, gram = pl.pallas_call(
        functools.partial(gram_kernel, local * ring, [0] + steps),
        out_shape=(pltpu.VMEM((2, states, local), bf16), square),
        in_specs=[VMEM] * parts,
        out_specs=(VMEM, VMEM),
        compiler_params=ROOM,
        name="gram",
    )(*gathering)
    terms = [near(gram), exchange(near(gram), "nodes", 1)]
    bit = 2
    while bit < ring:
        total = near(
            pl.pallas_call(
                sum_kernel,
                out_shape=square,
                in_specs=[VMEM] * len(terms),
                out_specs=VMEM,
                compiler_params=ROOM,
                name="sum",
            )(*terms)
        )
        peers = [bit, 2 * bit, 3 * bit] if 2 * bit < ring else [bit]
        terms = [total] + [exchange(total, "nodes", k) for k in peers]
        bit *= 4
    return pl.pallas_call(
        rotate_kernel,
        out_shape=jax.ShapeDtypeStruct((rows, local), f32),
        in_specs=[VMEM] * (len(terms) + 1),
        out_specs=VMEM,
        scratch_shapes=[square, square],
        compiler_params=ROOM,
        name="rotate",
    )(*terms, near(gathered))


def solution(mesh):
    placed = (P("states", "nodes"), P("nodes", None, None), P("nodes", None), P(), P())
    return jax.shard_map(
        on_device, mesh=mesh, in_specs=placed, out_specs=P("states", "nodes"), check_vma=False
    )
```

```python
import functools

import jax
import jax.numpy as jnp
from jax import lax
from jax.experimental import pallas as pl
from jax.experimental.pallas import tpu as pltpu
from jax.sharding import PartitionSpec as P

REACH = 4
LANES = 128
PANEL = 16
VMEM = pl.BlockSpec(memory_space=pltpu.VMEM)
SMEM = pl.BlockSpec(memory_space=pltpu.SMEM)
HBM = pl.BlockSpec(memory_space=pltpu.HBM)
ROOM = pltpu.CompilerParams(vmem_limit_bytes=16 * 2**20)
NT = (((1,), (1,)), ((), ()))
TN = (((0,), (0,)), ((), ()))


def halves(x):
    high = x.astype(jnp.bfloat16)
    return high, (x - high.astype(jnp.float32)).astype(jnp.bfloat16)


def stacked(x):
    return jnp.concatenate(halves(x), axis=0)


def swapped(tile):
    half = LANES // 2
    return jnp.concatenate([tile[:, half:], tile[:, :half]], axis=1)


def prepare(there, offsets_there, near_band, far_band, blocks, offsets, sems, *sums):
    count = there.shape[0]
    rows = half_rows(True, count) + half_rows(False, count)
    copies = [pltpu.make_async_copy(offsets_there, offsets, sems.at[count])]
    copies += [
        pltpu.make_async_copy(there.at[b], blocks.at[r], sems.at[r]) for r, b in enumerate(rows)
    ]
    for copy in copies:
        copy.start()
    for one in sums:
        one[...] = jnp.zeros(one.shape, jnp.float32)
    for copy in copies:
        copy.wait()
    add_up(blocks, rows, offsets, sums)
    make_band(sums[:REACH], near_band)
    make_band(sums[REACH:], far_band)


def half_rows(is_near, count):
    begin = jnp.where(before_own(is_near), 0, count - REACH)
    return [begin + r for r in range(REACH)]


def add_up(blocks, rows, offsets, sums):
    _, size, depth = blocks.shape
    neighbours = depth // size
    half = size // 2
    low_lanes = lax.broadcasted_iota(jnp.int32, (half, LANES), 1) < size
    for k in range(0, neighbours, 2):
        for r, (b, one) in enumerate(zip(rows, sums, strict=True)):
            tile = blocks[r, :, k * size : min(k + 2, neighbours) * size]
            if tile.shape[1] < LANES:
                tile = jnp.concatenate([tile, jnp.zeros_like(tile)], axis=1)
            turned = swapped(tile).astype(jnp.float32)
            tile = tile.astype(jnp.float32)
            place = offsets[b, k] + REACH
            one[place] = one[place] + jnp.where(low_lanes, tile[:half], turned[half:])
            if k + 1 < neighbours:
                place = offsets[b, k + 1] + REACH
                one[place] = one[place] + jnp.where(low_lanes, turned[:half], tile[half:])


def make_band(sums, band):
    span, half, _ = sums[0].shape
    size = 2 * half
    low_lanes = lax.broadcasted_iota(jnp.int32, (half, LANES), 1) < size
    zero = jnp.zeros((half, LANES), jnp.float32)
    for r, one in enumerate(sums):
        folded = [one[p] for p in range(span)]
        turned = [swapped(x) for x in folded]
        for t in range(3 * REACH // 2):
            low, high = 2 * t - r, 2 * t + 1 - r
            even, even_turned = (folded[low], turned[low]) if 0 <= low < span else (zero, zero)
            odd, odd_turned = (folded[high], turned[high]) if 0 <= high < span else (zero, zero)
            whole = jnp.concatenate(
                [jnp.where(low_lanes, even, odd_turned), jnp.where(low_lanes, even_turned, odd)], axis=0
            )
            top, rest = halves(whole)
            place = (slice(r * size, (r + 1) * size), slice(t * LANES, (t + 1) * LANES))
            band[(0, *place)] = top
            band[(1, *place)] = rest


def side(field, before):
    half = field.shape[1] // 2
    return jnp.where(before, field[:, :half], field[:, half:])


def joined(near, far, odd):
    return jnp.concatenate([jnp.where(odd, near, far), jnp.where(odd, far, near)], axis=1)


def before_own(is_near):
    odd = lax.axis_index("nodes") % 2
    return odd == (1 if is_near else 0)


def window(own, rim, before):
    wide = rim.shape[1]
    return jnp.concatenate(
        [
            jnp.where(before, rim, own[:, :wide]),
            jnp.where(before, own[:, :wide], own[:, wide:]),
            jnp.where(before, own[:, wide:], rim),
        ],
        axis=1,
    )


def apply_band(field, band):
    rows = field.shape[0]
    field = stacked(field)
    both = lax.dot_general(field, band[0], NT, preferred_element_type=jnp.float32)
    rest = lax.dot_general(field[:rows], band[1], NT, preferred_element_type=jnp.float32)
    return both[:rows] + (both[rows:] + rest)


def first_half(is_near, rim, own, band):
    before = before_own(is_near)
    return apply_band(window(own[...], side(rim[...], jnp.logical_not(before)), before), band)


def first_near(rim, own, band, out):
    out[...] = first_half(True, rim, own, band)


def first_far(rim, own, band, out):
    out[...] = first_half(False, rim, own, band)


def second_half(is_near, rim, near, far, band, earlier_rim, earlier, center, width):
    before = before_own(is_near)
    shift, scale = center[0], 1.0 / width[0]
    applied = window(joined(near[...], far[...], before_own(True)), rim[...], before)
    field = earlier[...]
    states = window(field, side(earlier_rim[...], jnp.logical_not(before)), before)
    first = (applied - shift * states) * scale
    half = rim.shape[1]
    mine = first[:, half : 2 * half]
    return 2.0 * ((apply_band(first, band) - shift * mine) * scale) - side(field, before)


def second_near(*refs):
    refs[-1][...] = second_half(True, *refs[:-1])


def second_far(*refs):
    *rest, done, out = refs
    out[...] = joined(done[...], second_half(False, *rest), before_own(True))


def gram_kernel(total_nodes, steps, *refs):
    parts, (gathered, gram) = refs[:-2], refs[-2:]
    rows = parts[0].shape[0]
    me = lax.axis_index("states")
    for step, part in zip(steps, parts, strict=True):
        place = pl.ds(pl.multiple_of((me ^ step) * rows, rows), rows)
        high, low = halves(part[...])
        gathered[0, place] = high
        gathered[1, place] = low
    states = len(parts) * rows
    both = gathered[...].reshape(2 * states, -1)
    terms = lax.dot_general(both, both, NT, preferred_element_type=jnp.float32)
    gram[...] = (terms[:states, :states] + (terms[:states, states:] + terms[states:, :states])) * (
        1.0 / total_nodes
    )


def sum_kernel(*refs):
    refs[-1][...] = functools.reduce(jnp.add, [ref[...] for ref in refs[:-1]])


def thirds(x):
    high = x.astype(jnp.bfloat16)
    rest = x - high.astype(jnp.float32)
    middle = rest.astype(jnp.bfloat16)
    return high, middle, (rest - middle.astype(jnp.float32)).astype(jnp.bfloat16)


def outer(left, right):
    a, b, c = thirds(left)
    d, e, f = thirds(right)
    return lax.dot_general(
        jnp.concatenate([a, a, b, a, b, c], axis=0),
        jnp.concatenate([d, e, d, f, e, d], axis=0),
        TN,
        preferred_element_type=jnp.float32,
    )


def inverse_factor(matrix, inverse):
    order = matrix.shape[0]
    lane = lax.broadcasted_iota(jnp.int32, (8, order), 1)
    sub = lax.broadcasted_iota(jnp.int32, (8, order), 0)
    carried = [matrix[i : i + 8] for i in range(0, PANEL, 8)]
    for start in range(0, order, PANEL):
        stop = start + PANEL
        after = min(stop + PANEL, order)
        groups = carried + [matrix[i : i + 8] for i in range(stop, after, 8)]
        inside = (lane >= start) & (lane < stop)
        columns = [
            [jnp.broadcast_to(g[:, k : k + 1], g.shape) for g in groups] for k in range(start, stop)
        ]
        for i, g in enumerate(groups):
            unit = jnp.where(lane == sub + (start + 8 * i), 1.0, 0.0) if 8 * i < PANEL else 0.0
            groups[i] = jnp.where(inside, unit, g)
        for j in range(PANEL):
            own, s = divmod(j, 8)
            scale = lax.rsqrt(columns[j][own][s : s + 1])
            pivot = groups[own][s : s + 1] * scale
            heads = [column[own][s : s + 1] * scale for column in columns]
            for i in range(own, len(groups)):
                factor = columns[j][i] * scale
                less = groups[i] - factor * pivot
                if i == own:
                    less = jnp.where(sub > s, less, jnp.where(sub == s, pivot, groups[i]))
                groups[i] = less
                if i > own or s < 7:
                    for k in range(j + 1, PANEL):
                        columns[k][i] = columns[k][i] - factor * heads[k]
        rows, carried = jnp.concatenate(groups[: PANEL // 8], axis=0), groups[PANEL // 8 :]
        right = lax.broadcasted_iota(jnp.int32, rows.shape, 1) >= stop
        inverse[start:stop] = jnp.where(right, 0.0, rows)
        if after < order:
            update = outer(jnp.where(right, rows, 0.0), rows)
            rest = matrix[after:]
            at = lax.broadcasted_iota(jnp.int32, rest.shape, 1)
            kept = jnp.where((at >= start) & (at < stop), 0.0, rest)
            matrix[after:] = kept - update[after:]


def rotate_kernel(*refs):
    *grams, gathered, out, matrix, inverse = refs
    matrix[...] = functools.reduce(jnp.add, [gram[...] for gram in grams])
    inverse_factor(matrix, inverse)
    rows = out.shape[0]
    me = lax.axis_index("states")
    high, low = halves(inverse[pl.ds(pl.multiple_of(me * rows, rows), rows)])
    both = lax.dot_general(
        jnp.concatenate([high, low], axis=0),
        gathered[0],
        (((1,), (0,)), ((), ())),
        preferred_element_type=jnp.float32,
    )
    rest = jnp.dot(high, gathered[1], preferred_element_type=jnp.float32)
    out[...] = both[:rows] + (both[rows:] + rest)


def near(x):
    return pltpu.with_memory_space_constraint(x, pltpu.VMEM)


def there(x):
    return pltpu.with_memory_space_constraint(x, pltpu.HBM)


def exchange(x, axis, step):
    count = lax.axis_size(axis)
    return near(lax.ppermute(x, axis, [(i, i ^ step) for i in range(count)]))


def on_device(states_block, hamiltonian, offsets, center, halfwidth):
    rows, local = states_block.shape
    count, size, depth = hamiltonian.shape
    half = local // 2
    ring = lax.axis_size("nodes")
    parts = lax.axis_size("states")
    states = rows * parts
    off_chip = [(i, (i + 1 if i % 2 else i - 1) % ring) for i in range(ring)]
    f32, bf16 = jnp.float32, jnp.bfloat16
    field = pltpu.VMEM((rows, local), f32)
    part = pltpu.VMEM((rows, half), f32)
    square = pltpu.VMEM((states, states), f32)
    band = pltpu.VMEM((2, REACH * size, 3 * REACH * size), bf16)
    sums = pltpu.VMEM((2 * REACH + 1, size // 2, LANES), f32)

    def over_links(x):
        return near(lax.ppermute(x, "nodes", off_chip))

    def call(kernel, out, *operands, name):
        return near(
            pl.pallas_call(
                kernel,
                out_shape=out,
                in_specs=[SMEM if x.size == 1 else VMEM for x in operands],
                out_specs=VMEM,
                compiler_params=ROOM,
                name=name,
            )(*operands)
        )

    far_states = over_links(states_block)
    near_states = exchange(states_block, "nodes", 1)
    near_band, far_band = pl.pallas_call(
        prepare,
        out_shape=(band, band),
        in_specs=[HBM, HBM],
        out_specs=(VMEM, VMEM),
        scratch_shapes=[
            pltpu.VMEM(hamiltonian.shape, bf16),
            pltpu.SMEM(offsets.shape, jnp.int32),
            pltpu.SemaphoreType.DMA((count + 1,)),
            *[sums] * count,
        ],
        compiler_params=ROOM,
        name="prepare",
    )(there(hamiltonian), there(offsets))
    near_band, far_band = near(near_band), near(far_band)
    own = near(states_block)
    near_part = call(first_near, part, near_states, own, near_band, name="first_near")
    near_rim = exchange(near_part, "nodes", 1)
    far_part = call(first_far, part, far_states, own, far_band, name="first_far")
    far_rim = over_links(far_part)
    parts_of = (near_part, far_part)
    scalars = (center, halfwidth)
    near_second = call(
        second_near, part, near_rim, *parts_of, near_band, near_states, own, *scalars, name="second_near"
    )
    second = call(
        second_far,
        field,
        far_rim,
        *parts_of,
        far_band,
        far_states,
        own,
        *scalars,
        near_second,
        name="second_far",
    )
    steps = sorted(range(1, parts), key=lambda k: (k % 2, k))
    gathering = [second] + [exchange(second, "states", k) for k in steps]
    gathered, gram = pl.pallas_call(
        functools.partial(gram_kernel, local * ring, [0] + steps),
        out_shape=(pltpu.VMEM((2, states, local), bf16), square),
        in_specs=[VMEM] * parts,
        out_specs=(VMEM, VMEM),
        compiler_params=ROOM,
        name="gram",
    )(*gathering)
    terms = [near(gram), exchange(near(gram), "nodes", 1)]
    bit = 2
    while bit < ring:
        total = near(
            pl.pallas_call(
                sum_kernel,
                out_shape=square,
                in_specs=[VMEM] * len(terms),
                out_specs=VMEM,
                compiler_params=ROOM,
                name="sum",
            )(*terms)
        )
        peers = [bit, 2 * bit, 3 * bit] if 2 * bit < ring else [bit]
        terms = [total] + [exchange(total, "nodes", k) for k in peers]
        bit *= 4
    return pl.pallas_call(
        rotate_kernel,
        out_shape=jax.ShapeDtypeStruct((rows, local), f32),
        in_specs=[VMEM] * (len(terms) + 1),
        out_specs=VMEM,
        scratch_shapes=[square, square],
        compiler_params=ROOM,
        name="rotate",
    )(*terms, near(gathered))


def solution(mesh):
    placed = (P("states", "nodes"), P("nodes", None, None), P("nodes", None), P(), P())
    return jax.shard_map(
        on_device, mesh=mesh, in_specs=placed, out_specs=P("states", "nodes"), check_vma=False
    )
```

```python
import functools

import jax
import jax.numpy as jnp
from jax import lax
from jax.experimental import pallas as pl
from jax.experimental.pallas import tpu as pltpu
from jax.sharding import PartitionSpec as P

REACH = 4
LANES = 128
PANEL = 16
VMEM = pl.BlockSpec(memory_space=pltpu.VMEM)
SMEM = pl.BlockSpec(memory_space=pltpu.SMEM)
HBM = pl.BlockSpec(memory_space=pltpu.HBM)
ROOM = pltpu.CompilerParams(vmem_limit_bytes=16 * 2**20)
NT = (((1,), (1,)), ((), ()))
TN = (((0,), (0,)), ((), ()))


def halves(x):
    high = x.astype(jnp.bfloat16)
    return high, (x - high.astype(jnp.float32)).astype(jnp.bfloat16)


def stacked(x):
    return jnp.concatenate(halves(x), axis=0)


def swapped(tile):
    half = LANES // 2
    return jnp.concatenate([tile[:, half:], tile[:, :half]], axis=1)


def prepare(there, offsets_there, near_band, far_band, blocks, offsets, sems, *sums):
    count = there.shape[0]
    rows = half_rows(True, count) + half_rows(False, count)
    copies = [pltpu.make_async_copy(offsets_there, offsets, sems.at[count])]
    copies += [
        pltpu.make_async_copy(there.at[b], blocks.at[r], sems.at[r]) for r, b in enumerate(rows)
    ]
    for copy in copies:
        copy.start()
    for one in sums:
        one[...] = jnp.zeros(one.shape, jnp.float32)
    for copy in copies:
        copy.wait()
    add_up(blocks, rows, offsets, sums)
    make_band(sums[:REACH], near_band)
    make_band(sums[REACH:], far_band)


def half_rows(is_near, count):
    begin = jnp.where(before_own(is_near), 0, count - REACH)
    return [begin + r for r in range(REACH)]


def add_up(blocks, rows, offsets, sums):
    _, size, depth = blocks.shape
    neighbours = depth // size
    half = size // 2
    low_lanes = lax.broadcasted_iota(jnp.int32, (half, LANES), 1) < size
    for k in range(0, neighbours, 2):
        for r, (b, one) in enumerate(zip(rows, sums, strict=True)):
            tile = blocks[r, :, k * size : min(k + 2, neighbours) * size]
            if tile.shape[1] < LANES:
                tile = jnp.concatenate([tile, jnp.zeros_like(tile)], axis=1)
            turned = swapped(tile).astype(jnp.float32)
            tile = tile.astype(jnp.float32)
            place = offsets[b, k] + REACH
            one[place] = one[place] + jnp.where(low_lanes, tile[:half], turned[half:])
            if k + 1 < neighbours:
                place = offsets[b, k + 1] + REACH
                one[place] = one[place] + jnp.where(low_lanes, turned[:half], tile[half:])


def make_band(sums, band):
    span, half, _ = sums[0].shape
    size = 2 * half
    low_lanes = lax.broadcasted_iota(jnp.int32, (half, LANES), 1) < size
    zero = jnp.zeros((half, LANES), jnp.float32)
    for r, one in enumerate(sums):
        folded = [one[p] for p in range(span)]
        turned = [swapped(x) for x in folded]
        for t in range(3 * REACH // 2):
            low, high = 2 * t - r, 2 * t + 1 - r
            even, even_turned = (folded[low], turned[low]) if 0 <= low < span else (zero, zero)
            odd, odd_turned = (folded[high], turned[high]) if 0 <= high < span else (zero, zero)
            whole = jnp.concatenate(
                [jnp.where(low_lanes, even, odd_turned), jnp.where(low_lanes, even_turned, odd)], axis=0
            )
            top, rest = halves(whole)
            place = (slice(r * size, (r + 1) * size), slice(t * LANES, (t + 1) * LANES))
            band[(0, *place)] = top
            band[(1, *place)] = rest


def side(field, before):
    half = field.shape[1] // 2
    return jnp.where(before, field[:, :half], field[:, half:])


def joined(near, far, odd):
    return jnp.concatenate([jnp.where(odd, near, far), jnp.where(odd, far, near)], axis=1)


def before_own(is_near):
    odd = lax.axis_index("nodes") % 2
    return odd == (1 if is_near else 0)


def window(own, rim, before):
    wide = rim.shape[1]
    return jnp.concatenate(
        [
            jnp.where(before, rim, own[:, :wide]),
            jnp.where(before, own[:, :wide], own[:, wide:]),
            jnp.where(before, own[:, wide:], rim),
        ],
        axis=1,
    )


def apply_band(field, band):
    rows = field.shape[0]
    field = stacked(field)
    both = lax.dot_general(field, band[0], NT, preferred_element_type=jnp.float32)
    rest = lax.dot_general(field[:rows], band[1], NT, preferred_element_type=jnp.float32)
    return both[:rows] + (both[rows:] + rest)


def first_half(is_near, rim, own, band):
    before = before_own(is_near)
    return apply_band(window(own[...], side(rim[...], jnp.logical_not(before)), before), band)


def first_near(rim, own, band, out):
    out[...] = first_half(True, rim, own, band)


def first_far(rim, own, band, out):
    out[...] = first_half(False, rim, own, band)


def second_half(is_near, rim, near, far, band, earlier_rim, earlier, center, width):
    before = before_own(is_near)
    shift, scale = center[0], 1.0 / width[0]
    applied = window(joined(near[...], far[...], before_own(True)), rim[...], before)
    field = earlier[...]
    states = window(field, side(earlier_rim[...], jnp.logical_not(before)), before)
    first = (applied - shift * states) * scale
    half = rim.shape[1]
    mine = first[:, half : 2 * half]
    return 2.0 * ((apply_band(first, band) - shift * mine) * scale) - side(field, before)


def second_near(*refs):
    refs[-1][...] = second_half(True, *refs[:-1])


def second_far(*refs):
    *rest, done, out = refs
    out[...] = stacked(joined(done[...], second_half(False, *rest), before_own(True)))


def gram_kernel(total_nodes, steps, *refs):
    parts, (gathered, gram) = refs[:-2], refs[-2:]
    rows = parts[0].shape[0] // 2
    me = lax.axis_index("states")
    for step, part in zip(steps, parts, strict=True):
        place = pl.ds(pl.multiple_of((me ^ step) * rows, rows), rows)
        gathered[0, place] = part[:rows]
        gathered[1, place] = part[rows:]
    states = len(parts) * rows
    both = gathered[...].reshape(2 * states, -1)
    terms = lax.dot_general(both, both, NT, preferred_element_type=jnp.float32)
    gram[...] = (terms[:states, :states] + (terms[:states, states:] + terms[states:, :states])) * (
        1.0 / total_nodes
    )


def sum_kernel(*refs):
    refs[-1][...] = functools.reduce(jnp.add, [ref[...] for ref in refs[:-1]])


def thirds(x):
    high = x.astype(jnp.bfloat16)
    rest = x - high.astype(jnp.float32)
    middle = rest.astype(jnp.bfloat16)
    return high, middle, (rest - middle.astype(jnp.float32)).astype(jnp.bfloat16)


def outer(left, right):
    a, b, c = thirds(left)
    d, e, f = thirds(right)
    return lax.dot_general(
        jnp.concatenate([a, a, b, a, b, c], axis=0),
        jnp.concatenate([d, e, d, f, e, d], axis=0),
        TN,
        preferred_element_type=jnp.float32,
    )


def inverse_factor(matrix, inverse):
    order = matrix.shape[0]
    lane = lax.broadcasted_iota(jnp.int32, (8, order), 1)
    sub = lax.broadcasted_iota(jnp.int32, (8, order), 0)
    carried = [matrix[i : i + 8] for i in range(0, PANEL, 8)]
    for start in range(0, order, PANEL):
        stop = start + PANEL
        after = min(stop + PANEL, order)
        groups = carried + [matrix[i : i + 8] for i in range(stop, after, 8)]
        inside = (lane >= start) & (lane < stop)
        columns = [
            [jnp.broadcast_to(g[:, k : k + 1], g.shape) for g in groups] for k in range(start, stop)
        ]
        for i, g in enumerate(groups):
            unit = jnp.where(lane == sub + (start + 8 * i), 1.0, 0.0) if 8 * i < PANEL else 0.0
            groups[i] = jnp.where(inside, unit, g)
        for j in range(PANEL):
            own, s = divmod(j, 8)
            scale = lax.rsqrt(columns[j][own][s : s + 1])
            pivot = groups[own][s : s + 1] * scale
            heads = [column[own][s : s + 1] * scale for column in columns]
            for i in range(own, len(groups)):
                factor = columns[j][i] * scale
                less = groups[i] - factor * pivot
                if i == own:
                    less = jnp.where(sub > s, less, jnp.where(sub == s, pivot, groups[i]))
                groups[i] = less
                if i > own or s < 7:
                    for k in range(j + 1, PANEL):
                        columns[k][i] = columns[k][i] - factor * heads[k]
        rows, carried = jnp.concatenate(groups[: PANEL // 8], axis=0), groups[PANEL // 8 :]
        right = lax.broadcasted_iota(jnp.int32, rows.shape, 1) >= stop
        inverse[start:stop] = jnp.where(right, 0.0, rows)
        if after < order:
            update = outer(jnp.where(right, rows, 0.0), rows)
            rest = matrix[after:]
            at = lax.broadcasted_iota(jnp.int32, rest.shape, 1)
            kept = jnp.where((at >= start) & (at < stop), 0.0, rest)
            matrix[after:] = kept - update[after:]


def rotate_kernel(*refs):
    *grams, gathered, out, matrix, inverse = refs
    matrix[...] = functools.reduce(jnp.add, [gram[...] for gram in grams])
    inverse_factor(matrix, inverse)
    rows = out.shape[0]
    me = lax.axis_index("states")
    high, low = halves(inverse[pl.ds(pl.multiple_of(me * rows, rows), rows)])
    both = lax.dot_general(
        jnp.concatenate([high, low], axis=0),
        gathered[0],
        (((1,), (0,)), ((), ())),
        preferred_element_type=jnp.float32,
    )
    rest = jnp.dot(high, gathered[1], preferred_element_type=jnp.float32)
    out[...] = both[:rows] + (both[rows:] + rest)


def near(x):
    return pltpu.with_memory_space_constraint(x, pltpu.VMEM)


def there(x):
    return pltpu.with_memory_space_constraint(x, pltpu.HBM)


def exchange(x, axis, step):
    count = lax.axis_size(axis)
    return near(lax.ppermute(x, axis, [(i, i ^ step) for i in range(count)]))


def on_device(states_block, hamiltonian, offsets, center, halfwidth):
    rows, local = states_block.shape
    count, size, depth = hamiltonian.shape
    half = local // 2
    ring = lax.axis_size("nodes")
    parts = lax.axis_size("states")
    states = rows * parts
    off_chip = [(i, (i + 1 if i % 2 else i - 1) % ring) for i in range(ring)]
    f32, bf16 = jnp.float32, jnp.bfloat16
    field = pltpu.VMEM((rows, local), f32)
    part = pltpu.VMEM((rows, half), f32)
    square = pltpu.VMEM((states, states), f32)
    band = pltpu.VMEM((2, REACH * size, 3 * REACH * size), bf16)
    sums = pltpu.VMEM((2 * REACH + 1, size // 2, LANES), f32)

    def over_links(x):
        return near(lax.ppermute(x, "nodes", off_chip))

    def call(kernel, out, *operands, name):
        return near(
            pl.pallas_call(
                kernel,
                out_shape=out,
                in_specs=[SMEM if x.size == 1 else VMEM for x in operands],
                out_specs=VMEM,
                compiler_params=ROOM,
                name=name,
            )(*operands)
        )

    far_states = over_links(states_block)
    near_states = exchange(states_block, "nodes", 1)
    near_band, far_band = pl.pallas_call(
        prepare,
        out_shape=(band, band),
        in_specs=[HBM, HBM],
        out_specs=(VMEM, VMEM),
        scratch_shapes=[
            pltpu.VMEM(hamiltonian.shape, bf16),
            pltpu.SMEM(offsets.shape, jnp.int32),
            pltpu.SemaphoreType.DMA((count + 1,)),
            *[sums] * count,
        ],
        compiler_params=ROOM,
        name="prepare",
    )(there(hamiltonian), there(offsets))
    near_band, far_band = near(near_band), near(far_band)
    own = near(states_block)
    near_part = call(first_near, part, near_states, own, near_band, name="first_near")
    near_rim = exchange(near_part, "nodes", 1)
    far_part = call(first_far, part, far_states, own, far_band, name="first_far")
    far_rim = over_links(far_part)
    parts_of = (near_part, far_part)
    scalars = (center, halfwidth)
    near_second = call(
        second_near, part, near_rim, *parts_of, near_band, near_states, own, *scalars, name="second_near"
    )
    second = call(
        second_far,
        pltpu.VMEM((2 * rows, local), bf16),
        far_rim,
        *parts_of,
        far_band,
        far_states,
        own,
        *scalars,
        near_second,
        name="second_far",
    )
    steps = sorted(range(1, parts), key=lambda k: (k % 2, k))
    gathering = [second] + [exchange(second, "states", k) for k in steps]
    gathered, gram = pl.pallas_call(
        functools.partial(gram_kernel, local * ring, [0] + steps),
        out_shape=(pltpu.VMEM((2, states, local), bf16), square),
        in_specs=[VMEM] * parts,
        out_specs=(VMEM, VMEM),
        compiler_params=ROOM,
        name="gram",
    )(*gathering)
    terms = [near(gram), exchange(near(gram), "nodes", 1)]
    bit = 2
    while bit < ring:
        total = near(
            pl.pallas_call(
                sum_kernel,
                out_shape=square,
                in_specs=[VMEM] * len(terms),
                out_specs=VMEM,
                compiler_params=ROOM,
                name="sum",
            )(*terms)
        )
        peers = [bit, 2 * bit, 3 * bit] if 2 * bit < ring else [bit]
        terms = [total] + [exchange(total, "nodes", k) for k in peers]
        bit *= 4
    return pl.pallas_call(
        rotate_kernel,
        out_shape=jax.ShapeDtypeStruct((rows, local), f32),
        in_specs=[VMEM] * (len(terms) + 1),
        out_specs=VMEM,
        scratch_shapes=[square, square],
        compiler_params=ROOM,
        name="rotate",
    )(*terms, near(gathered))


def solution(mesh):
    placed = (P("states", "nodes"), P("nodes", None, None), P("nodes", None), P(), P())
    return jax.shard_map(
        on_device, mesh=mesh, in_specs=placed, out_specs=P("states", "nodes"), check_vma=False
    )
```
